32 devices in a mesh: grp: 2 (over y), tm: 4 (over z), spin: 2 (over core), rows: 2 (over x).
Axes of the slice: x: 2, y: 2, z: 4, core: 2. Of those that a mesh axis runs over, the one named last changes fastest.
Arguments:
- ising_field: int32 [32, 768], P(('grp', 'tm')), parts along dimension 0, may hold values from 0 to 1
- bond_sites: int32 [3072, 2], replicated, may hold values from 0 to 767
- hopping: float32 [3072], replicated, may hold values from 0.5 to 2
- tile_cols: int32 [6, 3], replicated, may hold values from 0 to 5, as said below
Outputs:
- xcorr: float32 [2, 8, 768, 768], P('spin', ('grp', 'tm'), None, 'rows'), parts along dimension 1
The draws below stay inside these ranges and needn't reach their ends.
There are 2 independent parts, one for each index of `grp`. The reference program is written for one: setup_inputs(seed, part) draws one part's arguments, and reference() takes and returns one part's arrays. A program takes and returns all parts, laid end to end along the dimension named above; an argument that names none is the same for every part. Nothing has to cross between parts.
Inputs may be any that keep to these rules, and one draw needn't show every extreme that they name: `ising_field`: 0 stands for the field value -1 and 1 for +1. `bond_sites`: A bond whose tile pair is not in tile_cols adds nothing to H, because tile_mask removes it; its entry in `hopping` is not zero. `tile_cols`: row r lists r first and then the two tiles beside r on a cycle through all 6 tiles drawn from the seed, so each tile row names 3 distinct tiles and the pattern is symmetric.
All inputs are finite; a program needn't handle non-finite values.
Results may differ from the reference program's by a relative error of at most 0.0003.
Values sent between devices are 32-bit elements; how exact they have to be, the bound alone decides.
A program may use at most 64 MiB of HBM per device.

```python
import math
import jax
import jax.numpy as jnp
from jax import lax

N = 768
NT = 6
BONDS = 3072
SL_DEV = 4
SLICES = 16
BLOCKS = 4


def draw_tile_cols(key, part):
    ordering = jax.random.permutation(key, NT).astype(jnp.int32)
    position = jnp.zeros((NT,), jnp.int32).at[ordering].set(jnp.arange(NT, dtype=jnp.int32))
    following = ordering[(position + 1) % NT]
    preceding = ordering[(position - 1 + NT) % NT]
    return jnp.stack([jnp.arange(NT, dtype=jnp.int32), following, preceding], axis=1).astype(jnp.int32)


def with_ends(array, own_key, smallest, largest):
    spot = [jax.random.randint(jax.random.fold_in(own_key, axis), (), 0, length) for axis, length in enumerate(array.shape)]
    longest = array.shape.index(max(array.shape))
    neighbour = spot[:longest] + [(spot[longest] + 1) % array.shape[longest]] + spot[longest + 1:]
    return array.at[tuple(spot)].set(smallest).at[tuple(neighbour)].set(largest)


def setup_inputs(seed: int = 0, part: int = 0) -> dict:
    key_list = jax.random.split(jax.random.key(seed), 5)
    own_keys = jax.random.split(jax.random.fold_in(key_list[4], part), 5)
    return {
        "ising_field": with_ends(jax.random.randint(own_keys[0], (SLICES, N), 0, 2), jax.random.fold_in(own_keys[0], 1), 0, 1).astype(jnp.int32),
        "bond_sites": with_ends(jax.random.randint(key_list[1], (BONDS, 2), 0, N), jax.random.fold_in(key_list[1], 1), 0, N - 1).astype(jnp.int32),
        "hopping": jnp.clip(jnp.exp(jax.random.uniform(key_list[2], (BONDS,), jnp.float32, math.log(0.5), math.log(2.0))), 0.5, 2.0),
        "tile_cols": draw_tile_cols(jax.random.fold_in(key_list[4], 71), part),
    }


def matmul_hi(left, right):
    return jnp.dot(left.astype(jnp.float32), right.astype(jnp.float32), precision=lax.Precision.HIGHEST, preferred_element_type=jnp.float32)

def build_kinetic(bond_sites, hopping, tile_cols, matrix_order, hop_scale):
    n_tiles = tile_cols.shape[0]
    tile_len = matrix_order // n_tiles
    tile_mask = jnp.any(tile_cols[:, :, None] == jnp.arange(n_tiles, dtype=jnp.int32)[None, None, :], axis=1).astype(jnp.float32)
    site_from = bond_sites[:, 0]
    site_to = bond_sites[:, 1]
    kept_mask = tile_mask[site_from // tile_len, site_to // tile_len]
    weights = hopping * kept_mask
    hop_matrix = jnp.zeros((matrix_order, matrix_order), jnp.float32)
    hop_matrix = hop_matrix.at[site_from, site_to].add(weights).at[site_to, site_from].add(weights)
    return jnp.eye(matrix_order, dtype=jnp.float32) + hop_scale * hop_matrix

def reference(ising_field, bond_sites, hopping, tile_cols):
    kinetic = build_kinetic(bond_sites, hopping, tile_cols, N, 0.5 / SLICES)
    coupling = 1.5 / math.sqrt(SLICES)
    spins_pm = (2 * ising_field - 1).astype(jnp.float32)
    identity = jnp.eye(N, dtype=jnp.float32)
    greens = []
    for spin_sign in (1.0, -1.0):
        factors = jnp.exp(spin_sign * coupling * spins_pm).reshape(BLOCKS, SL_DEV, N)

        def cluster_of(block_factors):

            def apply_slice(carry, slice_factors):
                return (slice_factors[:, None] * matmul_hi(kinetic, carry), None)
            result, _ = lax.scan(apply_slice, identity, block_factors)
            return result
        clusters = lax.map(cluster_of, factors)

        def cyclic_of(start):

            def apply_block(offset_step, carry):
                return matmul_hi(clusters[(start + offset_step) % BLOCKS], carry)
            return lax.fori_loop(0, BLOCKS, apply_block, identity)
        products = lax.map(cyclic_of, jnp.arange(BLOCKS, dtype=jnp.int32))

        def green_of(product):
            col_max = jnp.max(lax.optimization_barrier(jnp.sum(product, axis=0)))
            power = product / (2.0 * col_max)
            return jnp.linalg.solve(identity + power, identity)
        greens.append(lax.map(green_of, products))
    green_up, green_down = greens
    first = green_up * (identity - jnp.swapaxes(green_down, 1, 2))
    second = green_down * (identity - jnp.swapaxes(green_up, 1, 2))
    return jnp.stack([first, second])
```

```python
import functools
import math

import jax
import jax.numpy as jnp
from jax import lax
from jax.experimental import pallas as pl
from jax.experimental.pallas import tpu as pltpu
from jax.sharding import PartitionSpec as P

BF16 = jnp.bfloat16
F32 = jnp.float32
VMEM_BYTES = 48 * 1024 * 1024


def split(x):
    high = x.astype(BF16)
    return high, (x - high.astype(F32)).astype(BF16)


def dot(left, right):
    return jnp.dot(left, right, preferred_element_type=F32)


def cycle_order(tile_cols, n_tiles):
    order = [jnp.int32(0), tile_cols[0, 1]]
    for _ in range(n_tiles - 2):
        here = order[-1]
        order.append(tile_cols[here, 1] + tile_cols[here, 2] - order[-2])

    def place(tile):
        found = jnp.int32(0)
        for position, name in enumerate(order):
            found = jnp.where(name == tile, jnp.int32(position), found)
        return found

    return order, place


def kinetic_kernel(
    n_tiles, tile_len, hop_scale, chunk, tile_cols, sites, hopping, k_high, k_low, one_hot, w_high, w_low, total
):
    bonds = sites.shape[1]
    pairs = n_tiles // 2
    wide = 2 * tile_len
    order, _ = cycle_order(tile_cols, n_tiles)
    total[...] = jnp.zeros_like(total)
    row_ids = lax.broadcasted_iota(jnp.int32, (tile_len, chunk), 0)
    lane_ids = lax.broadcasted_iota(jnp.int32, (tile_len, tile_len), 1)

    def add_chunk(step, carry):
        begin = pl.multiple_of(step * chunk, chunk)
        site_from = sites[0:1, pl.ds(begin, chunk)]
        for p in range(n_tiles):
            hits = jnp.where(row_ids + order[p] * tile_len == site_from, 1.0, 0.0).astype(BF16)
            spots = [p + 1]
            if p == n_tiles - 1:
                spots.append(0)
            if p == 0:
                spots.append(n_tiles + 1)
            for spot in spots:
                one_hot[spot * tile_len : (spot + 1) * tile_len, :] = hits
        for part in range(chunk // tile_len):
            at = pl.multiple_of(begin + part * tile_len, tile_len)
            inside = slice(part * tile_len, (part + 1) * tile_len)
            site_to = jnp.broadcast_to(sites[1:2, pl.ds(at, tile_len)], (tile_len, tile_len)).T
            weight = jnp.broadcast_to(hopping[0:1, pl.ds(at, tile_len)], (tile_len, tile_len)).T
            high = weight.astype(BF16).astype(F32)
            low = weight - high
            for p in range(n_tiles):
                hit = lane_ids + order[p] * tile_len == site_to
                columns = slice(p * tile_len, (p + 1) * tile_len)
                w_high[inside, columns] = jnp.where(hit, high, 0.0).astype(BF16)
                w_low[inside, columns] = jnp.where(hit, low, 0.0).astype(BF16)
        for r in range(pairs):
            rows = slice(r * wide, (r + 2) * wide)
            columns = slice(r * wide, (r + 1) * wide)
            found = one_hot[rows, :]
            total[r] += dot(found, w_high[:, columns]) + dot(found, w_low[:, columns])
        return carry

    lax.fori_loop(0, bonds // chunk, add_chunk, 0)

    def tile_of(p, q):
        r, half = divmod(q, 2)
        row = (p - (2 * r - 1)) % n_tiles
        return r, slice(row * tile_len, (row + 1) * tile_len), slice(half * tile_len, (half + 1) * tile_len)

    diagonal = lax.broadcasted_iota(jnp.int32, (tile_len, tile_len), 0) == lane_ids
    k_high[...] = jnp.zeros_like(k_high)
    k_low[...] = jnp.zeros_like(k_low)
    for q in range(n_tiles):
        for p in ((q - 1) % n_tiles, q, (q + 1) % n_tiles):
            value = hop_scale * (total[tile_of(p, q)] + total[tile_of(q, p)].T)
            if p == q:
                value = jnp.where(diagonal, 1.0, 0.0) + value
            high, low = split(value)
            k_high[tile_of(p, q)] = high
            k_low[tile_of(p, q)] = low


def green_kernel(
    n_tiles, tile_len, slices_here, coupling, width,
    tile_cols, field, k_high, k_low, mine, sent,
    factors, y_high, y_low, x_full, x_high, x_low, b_high, b_low, u_full, t_full,
):
    total_slices = field.shape[0]
    order_len = n_tiles * tile_len
    pairs = n_tiles // 2
    wide = 2 * tile_len
    order, place = cycle_order(tile_cols, n_tiles)
    spin_sign = 1.0 - 2.0 * lax.axis_index("spin").astype(F32)
    start = lax.axis_index("tm") * slices_here
    strength = spin_sign * coupling
    for p in range(n_tiles):
        spins_pm = (2 * field[:, pl.ds(pl.multiple_of(order[p] * tile_len, tile_len), tile_len)] - 1).astype(F32)
        factors[:, p * tile_len : (p + 1) * tile_len] = jnp.exp(strength * spins_pm)

    def keep(slot, r, value):
        parts = split(value)
        for ref, part in zip((y_high, y_low), parts):
            ref[slot, :, tile_len + r * wide : tile_len + (r + 1) * wide] = part
            if r == 0:
                ref[slot, :, tile_len + order_len : 2 * tile_len + order_len] = part[:, :tile_len]
            if r == pairs - 1:
                ref[slot, :, :tile_len] = part[:, tile_len:]

    first = factors[pl.ds(start, 1), :]
    for r in range(pairs):
        window = k_high[r].astype(F32) + k_low[r].astype(F32)
        rows = [jnp.zeros((tile_len, wide), F32)] * n_tiles
        for row in range(4):
            rows[(2 * r - 1 + row) % n_tiles] = window[row * tile_len : (row + 1) * tile_len]
        keep(0, r, jnp.concatenate(rows, axis=0) * first[:, r * wide : (r + 1) * wide])

    def slice_step(step, carry):
        old, new = lax.rem(step - 1, 2), lax.rem(step, 2)
        factor = factors[pl.ds(lax.rem(start + step, total_slices), 1), :]
        for r in range(pairs):
            window = slice(r * wide, (r + 2) * wide)
            high = y_high[old, :, window]
            value = dot(high, k_high[r]) + dot(high, k_low[r]) + dot(y_low[old, :, window], k_high[r])
            keep(new, r, value * factor[:, r * wide : (r + 1) * wide])
        return carry

    lax.fori_loop(1, total_slices, slice_step, 0)
    last = (total_slices - 1) % 2
    inner = slice(tile_len, tile_len + order_len)
    product = y_high[last, :, inner].astype(F32) + y_low[last, :, inner].astype(F32)
    col_max = jnp.max(jnp.sum(product, axis=1))
    power = product * (-0.5 / col_max)
    x_full[...] = power
    high, low = split(power)
    x_high[...] = high
    x_low[...] = low

    bands = [slice(r * wide, (r + 1) * wide) for r in range(pairs)]
    second = (y_high.at[0, :, inner], y_low.at[0, :, inner])
    third = (y_high.at[1, :, inner], y_low.at[1, :, inner])

    def product3(left, right, band):
        l_high, l_low = left
        r_high, r_low = right
        return (
            dot(l_high[...], r_high[:, band]) + dot(l_high[...], r_low[:, band]) + dot(l_low[...], r_high[:, band])
        )

    def put(pair, band, value):
        pair[0][:, band], pair[1][:, band] = split(value)

    x = (x_high, x_low)
    for band in bands:
        value = product3(x, x, band)
        put(second, band, value)
        u_full[:, band] = x_full[:, band] + value
    for band in bands:
        value = product3(x, second, band)
        put(third, band, value)
        t_full[:, band] = value
    for band in bands:
        value = product3(third, third, band)
        b_high[:, band] = value.astype(BF16)
        both = t_full[:, band] + value
        t_full[:, band] = both
        second[0][:, band] = both.astype(BF16)
    for band in bands:
        value = dot(b_high[...], second[0][:, band])
        t_full[:, band] += value
        b_low[:, band] = value.astype(BF16)
    for band in bands:
        put(third, band, t_full[:, band] + dot(b_high[...], b_low[:, band]))
        put(x, band, u_full[:, band])
    for band in bands:
        rest = third[0][:, band].astype(F32) + third[1][:, band].astype(F32)
        x_full[:, band] = -(u_full[:, band] + rest + product3(x, third, band))

    base = lax.axis_index("rows") * (width // tile_len) if width < order_len else jnp.int32(0)
    spots = [pl.multiple_of(place(jnp.int32(a)) * tile_len, tile_len) for a in range(n_tiles)]
    for b in range(width // tile_len):
        spot = pl.multiple_of(place(base + b) * tile_len, tile_len)
        columns = slice(b * tile_len, (b + 1) * tile_len)
        for a in range(n_tiles):
            rows = slice(a * tile_len, (a + 1) * tile_len)
            sent[rows, columns] = x_full[pl.ds(spots[a], tile_len), pl.ds(spot, tile_len)]
            mine[rows, columns] = x_full[pl.ds(spot, tile_len), pl.ds(spots[a], tile_len)].T


def per_device(ising_field, bond_sites, hopping, tile_cols):
    slices_here, matrix_order = ising_field.shape
    n_tiles = tile_cols.shape[0]
    tile_len = matrix_order // n_tiles
    bonds = bond_sites.shape[0]
    n_rows = lax.axis_size("rows")
    col_width = matrix_order // n_rows
    total_slices = slices_here * lax.axis_size("tm")
    pairs = n_tiles // 2
    wide = 2 * tile_len
    extended = matrix_order + wide
    vmem = pl.BlockSpec(memory_space=pltpu.VMEM)
    smem = pl.BlockSpec(memory_space=pltpu.SMEM)
    square = (matrix_order, matrix_order)
    field = lax.all_gather(ising_field, "tm", axis=0, tiled=True)
    chunk = 4 * tile_len
    windows = jax.ShapeDtypeStruct((pairs, 2 * wide, wide), BF16)
    k_high, k_low = pl.pallas_call(
        functools.partial(kinetic_kernel, n_tiles, tile_len, 0.5 / total_slices, chunk),
        out_shape=(windows, windows),
        in_specs=[smem, vmem, vmem],
        out_specs=(vmem, vmem),
        scratch_shapes=[
            pltpu.VMEM((extended, chunk), BF16),
            pltpu.VMEM((chunk, matrix_order), BF16),
            pltpu.VMEM((chunk, matrix_order), BF16),
            pltpu.VMEM((pairs, 2 * wide, wide), F32),
        ],
        compiler_params=pltpu.CompilerParams(vmem_limit_bytes=VMEM_BYTES),
        cost_estimate=pl.CostEstimate(
            flops=4 * bonds * 2 * matrix_order * wide, bytes_accessed=4 * matrix_order * wide, transcendentals=0
        ),
        name="kinetic",
    )(tile_cols, bond_sites.T, hopping[None, :])
    width = col_width if col_width % tile_len == 0 else matrix_order
    half = jax.ShapeDtypeStruct((matrix_order, width), F32)
    mine, sent = pl.pallas_call(
        functools.partial(
            green_kernel, n_tiles, tile_len, slices_here, 1.5 / math.sqrt(total_slices), width
        ),
        out_shape=(half, half),
        in_specs=[smem, vmem, vmem, vmem],
        out_specs=(vmem, vmem),
        scratch_shapes=[pltpu.VMEM((total_slices, matrix_order), F32)]
        + [pltpu.VMEM((2, matrix_order, extended), BF16)] * 2
        + [pltpu.VMEM(square, F32)]
        + [pltpu.VMEM(square, BF16)] * 4
        + [pltpu.VMEM(square, F32)] * 2,
        compiler_params=pltpu.CompilerParams(vmem_limit_bytes=VMEM_BYTES),
        cost_estimate=pl.CostEstimate(
            flops=6 * total_slices * matrix_order * 2 * matrix_order * wide + 28 * matrix_order**3,
            bytes_accessed=8 * matrix_order * matrix_order,
            transcendentals=total_slices * matrix_order,
        ),
        name="green",
    )(tile_cols, field, k_high, k_low)
    offset = lax.axis_index("rows") * col_width
    if width != col_width:
        mine = lax.dynamic_slice_in_dim(mine, offset, col_width, 1)
        sent = lax.dynamic_slice_in_dim(sent, offset, col_width, 1)
    n_spin = lax.axis_size("spin")
    other = lax.ppermute(sent, "spin", [(i, n_spin - 1 - i) for i in range(n_spin)])
    row_ids = jnp.arange(matrix_order, dtype=jnp.int32)[:, None]
    col_ids = offset + jnp.arange(col_width, dtype=jnp.int32)[None, :]
    eye_cols = (row_ids == col_ids).astype(F32)
    xcorr = (eye_cols - mine) * other
    return xcorr[None, None]


def solution(mesh):
    placed = (P(("grp", "tm"), None), P(), P(), P())
    return jax.shard_map(
        per_device,
        mesh=mesh,
        in_specs=placed,
        out_specs=P("spin", ("grp", "tm"), None, "rows"),
        check_vma=False,
    )
```

```python
import functools
import math

import jax
import jax.numpy as jnp
from jax import lax
from jax.experimental import pallas as pl
from jax.experimental.pallas import tpu as pltpu
from jax.sharding import PartitionSpec as P

BF16 = jnp.bfloat16
F32 = jnp.float32
VMEM_BYTES = 48 * 1024 * 1024


def split(x):
    high = x.astype(BF16)
    return high, (x - high.astype(F32)).astype(BF16)


def dot(left, right):
    return jnp.dot(left, right, preferred_element_type=F32)


def cycle_order(tile_cols, n_tiles):
    order = [jnp.int32(0), tile_cols[1, 0]]
    for _ in range(n_tiles - 2):
        here = order[-1]
        order.append(tile_cols[1, here] + tile_cols[2, here] - order[-2])

    def place(tile):
        found = jnp.int32(0)
        for position, name in enumerate(order):
            found = jnp.where(name == tile, jnp.int32(position), found)
        return found

    return order, place


def kinetic_kernel(
    n_tiles, tile_len, hop_scale, chunk, tile_cols, sites, hopping, k_parts, one_hot, w_high, w_low, total
):
    bonds = sites.shape[1]
    pairs = n_tiles // 2
    wide = 2 * tile_len
    order, _ = cycle_order(tile_cols, n_tiles)
    row_ids = lax.broadcasted_iota(jnp.int32, (tile_len, chunk), 0)
    lane_ids = lax.broadcasted_iota(jnp.int32, (tile_len, tile_len), 1)

    def build(begin, slot):
        site_from = sites[0:1, begin : begin + chunk]
        for p in range(n_tiles):
            hits = jnp.where(row_ids + order[p] * tile_len == site_from, 1.0, 0.0).astype(BF16)
            spots = [p + 1]
            if p == n_tiles - 1:
                spots.append(0)
            if p == 0:
                spots.append(n_tiles + 1)
            for spot in spots:
                one_hot[slot, spot * tile_len : (spot + 1) * tile_len, :] = hits
        for part in range(chunk // tile_len):
            at = slice(begin + part * tile_len, begin + (part + 1) * tile_len)
            inside = slice(part * tile_len, (part + 1) * tile_len)
            site_to = jnp.broadcast_to(sites[1:2, at], (tile_len, tile_len)).T
            weight = jnp.broadcast_to(hopping[0:1, at], (tile_len, tile_len)).T
            high = weight.astype(BF16).astype(F32)
            low = weight - high
            for p in range(n_tiles):
                hit = lane_ids + order[p] * tile_len == site_to
                columns = slice(p * tile_len, (p + 1) * tile_len)
                w_high[slot, inside, columns] = jnp.where(hit, high, 0.0).astype(BF16)
                w_low[slot, inside, columns] = jnp.where(hit, low, 0.0).astype(BF16)

    build(0, 0)
    for begin in range(0, bonds, chunk):
        slot = begin // chunk % 2
        if begin + chunk < bonds:
            build(begin + chunk, 1 - slot)
        for r in range(pairs):
            columns = slice(r * wide, (r + 1) * wide)
            found = one_hot[slot, r * wide : (r + 2) * wide, :]
            weights = jnp.concatenate([w_high[slot, :, columns], w_low[slot, :, columns]], axis=0)
            added = dot(jnp.concatenate([found, found], axis=1), weights)
            total[r] = added if begin == 0 else total[r] + added

    def tile_of(p, q):
        r, half = divmod(q, 2)
        row = (p - (2 * r - 1)) % n_tiles
        return r, slice(row * tile_len, (row + 1) * tile_len), slice(half * tile_len, (half + 1) * tile_len)

    diagonal = lax.broadcasted_iota(jnp.int32, (tile_len, tile_len), 0) == lane_ids
    k_parts[...] = jnp.zeros_like(k_parts)
    for q in range(n_tiles):
        for p in ((q - 1) % n_tiles, q, (q + 1) % n_tiles):
            value = hop_scale * (total[tile_of(p, q)] + total[tile_of(q, p)].T)
            if p == q:
                value = jnp.where(diagonal, 1.0, 0.0) + value
            high, low = split(value)
            r, rows, columns = tile_of(p, q)
            for part, piece in enumerate((high, high, low)):
                k_parts[r, part * 2 * wide + rows.start : part * 2 * wide + rows.stop, columns] = piece


def green_kernel(
    n_tiles, tile_len, coupling, width,
    tile_cols, field, k_parts, mine, sent,
    factors, y_high, y_low, p_high, p_low, a_part, b_part, u_part, p_full, q_full,
):
    total_slices = field.shape[0]
    order_len = n_tiles * tile_len
    pairs = n_tiles // 2
    wide = 2 * tile_len
    order, place = cycle_order(tile_cols, n_tiles)
    strength = (1.0 - 2.0 * lax.axis_index("spin").astype(F32)) * coupling
    for p in range(n_tiles):
        spins_pm = (2 * field[:, pl.ds(pl.multiple_of(order[p] * tile_len, tile_len), tile_len)] - 1).astype(F32)
        factors[:, p * tile_len : (p + 1) * tile_len] = jnp.exp(strength * spins_pm)

    def keep(slot, r, value):
        parts = split(value)
        for ref, part in zip((y_high, y_low), parts):
            ref[slot, :, tile_len + r * wide : tile_len + (r + 1) * wide] = part
            if r == 0:
                ref[slot, :, tile_len + order_len : 2 * tile_len + order_len] = part[:, :tile_len]
            if r == pairs - 1:
                ref[slot, :, :tile_len] = part[:, tile_len:]

    for r in range(pairs):
        window = k_parts[r, : 2 * wide].astype(F32) + k_parts[r, 4 * wide :].astype(F32)
        rows = [jnp.zeros((tile_len, wide), F32)] * n_tiles
        for row in range(4):
            rows[(2 * r - 1 + row) % n_tiles] = window[row * tile_len : (row + 1) * tile_len]
        keep(0, r, jnp.concatenate(rows, axis=0) * factors[0:1, r * wide : (r + 1) * wide])

    def slice_step(step, carry):
        old, new = lax.rem(step - 1, 2), lax.rem(step, 2)
        factor = factors[pl.ds(step, 1), :]
        for r in range(pairs):
            window = slice(r * wide, (r + 2) * wide)
            high = y_high[old, :, window]
            value = dot(jnp.concatenate([high, y_low[old, :, window], high], axis=1), k_parts[r])
            keep(new, r, value * factor[:, r * wide : (r + 1) * wide])
        return carry

    lax.fori_loop(1, total_slices, slice_step, 0)
    last = (total_slices - 1) % 2
    inner = slice(tile_len, tile_len + order_len)
    product = y_high[last, :, inner].astype(F32) + y_low[last, :, inner].astype(F32)
    col_max = jnp.max(jnp.sum(product, axis=1))
    power = product * (0.5 / col_max)
    p_full[...] = power
    high, low = split(power)
    p_high[...] = high
    p_low[...] = low

    bands = [slice(r * wide, (r + 1) * wide) for r in range(pairs)]
    for band in bands:
        value = dot(p_high[...], p_high[:, band])
        a_part[:, band] = value.astype(BF16)
        value -= p_full[:, band]
        q_full[:, band] = value
        u_part[:, band] = value.astype(BF16)
    for band in bands:
        value = -dot(p_high[...], a_part[:, band])
        b_part[:, band] = value.astype(BF16)
    for band in bands:
        value = b_part[:, band].astype(F32) + dot(b_part[...], b_part[:, band])
        q_full[:, band] += value
        a_part[:, band] = value.astype(BF16)
    q_high, q_low = y_high.at[0, :, inner], y_low.at[0, :, inner]
    for band in bands:
        value = -(q_full[:, band] + dot(u_part[...], a_part[:, band]))
        q_full[:, band] = value
        q_high[:, band], q_low[:, band] = split(value)
    for band in bands:
        left = jnp.concatenate([p_high[...], p_low[...], p_high[...]], axis=1)
        right = jnp.concatenate([q_high[:, band], q_high[:, band], q_low[:, band]], axis=0)
        residual = dot(left, right) + (q_full[:, band] - p_full[:, band])
        a_part[:, band] = residual.astype(BF16)
        q_full[:, band] -= residual
    for band in bands:
        q_full[:, band] += dot(q_high[...], a_part[:, band])

    base = lax.axis_index("rows") * (width // tile_len) if width < order_len else jnp.int32(0)
    tile = (tile_len, tile_len)
    diagonal = lax.broadcasted_iota(jnp.int32, tile, 0) == lax.broadcasted_iota(jnp.int32, tile, 1)
    spots = [pl.multiple_of(place(jnp.int32(a)) * tile_len, tile_len) for a in range(n_tiles)]
    for b in range(width // tile_len):
        spot = pl.multiple_of(place(base + b) * tile_len, tile_len)
        columns = slice(b * tile_len, (b + 1) * tile_len)
        for a in range(n_tiles):
            rows = slice(a * tile_len, (a + 1) * tile_len)
            sent[rows, columns] = q_full[pl.ds(spots[a], tile_len), pl.ds(spot, tile_len)]
            unit = jnp.where(diagonal & (base + b == a), 1.0, 0.0)
            mine[rows, columns] = unit - q_full[pl.ds(spot, tile_len), pl.ds(spots[a], tile_len)].T


def per_device(ising_field, bond_sites, hopping, tile_cols):
    slices_here, matrix_order = ising_field.shape
    n_tiles = tile_cols.shape[0]
    tile_len = matrix_order // n_tiles
    bonds = bond_sites.shape[0]
    n_rows = lax.axis_size("rows")
    col_width = matrix_order // n_rows
    total_slices = slices_here * lax.axis_size("tm")
    pairs = n_tiles // 2
    wide = 2 * tile_len
    extended = matrix_order + wide
    vmem = pl.BlockSpec(memory_space=pltpu.VMEM)
    smem = pl.BlockSpec(memory_space=pltpu.SMEM)
    square = (matrix_order, matrix_order)
    n_time = lax.axis_size("tm")
    blocks = [ising_field]
    for ahead in range(1, n_time):
        blocks.append(lax.ppermute(ising_field, "tm", [(i, (i - ahead) % n_time) for i in range(n_time)]))
    field = jnp.concatenate(blocks, axis=0)
    chunk = 4 * tile_len
    k_parts = pl.pallas_call(
        functools.partial(kinetic_kernel, n_tiles, tile_len, 0.5 / total_slices, chunk),
        out_shape=jax.ShapeDtypeStruct((pairs, 6 * wide, wide), BF16),
        in_specs=[smem, vmem, vmem],
        out_specs=vmem,
        scratch_shapes=[
            pltpu.VMEM((2, extended, chunk), BF16),
            pltpu.VMEM((2, chunk, matrix_order), BF16),
            pltpu.VMEM((2, chunk, matrix_order), BF16),
            pltpu.VMEM((pairs, 2 * wide, wide), F32),
        ],
        compiler_params=pltpu.CompilerParams(vmem_limit_bytes=VMEM_BYTES),
        cost_estimate=pl.CostEstimate(
            flops=4 * bonds * 2 * matrix_order * wide, bytes_accessed=4 * matrix_order * wide, transcendentals=0
        ),
        name="kinetic",
    )(tile_cols.T, bond_sites.T, hopping[None, :])
    width = col_width if col_width % tile_len == 0 else matrix_order
    half = jax.ShapeDtypeStruct((matrix_order, width), F32)
    mine, sent = pl.pallas_call(
        functools.partial(
            green_kernel, n_tiles, tile_len, 1.5 / math.sqrt(total_slices), width
        ),
        out_shape=(half, half),
        in_specs=[smem, vmem, vmem],
        out_specs=(vmem, vmem),
        scratch_shapes=[pltpu.VMEM((total_slices, matrix_order), F32)]
        + [pltpu.VMEM((2, matrix_order, extended), BF16)] * 2
        + [pltpu.VMEM(square, BF16)] * 5
        + [pltpu.VMEM(square, F32)] * 2,
        compiler_params=pltpu.CompilerParams(vmem_limit_bytes=VMEM_BYTES),
        cost_estimate=pl.CostEstimate(
            flops=6 * total_slices * matrix_order * 2 * matrix_order * wide + 16 * matrix_order**3,
            bytes_accessed=8 * matrix_order * matrix_order,
            transcendentals=total_slices * matrix_order,
        ),
        name="green",
    )(tile_cols.T, field, k_parts)
    offset = lax.axis_index("rows") * col_width
    if width != col_width:
        mine = lax.dynamic_slice_in_dim(mine, offset, col_width, 1)
        sent = lax.dynamic_slice_in_dim(sent, offset, col_width, 1)
    n_spin = lax.axis_size("spin")
    other = lax.ppermute(sent, "spin", [(i, n_spin - 1 - i) for i in range(n_spin)])
    xcorr = mine * other
    return xcorr[None, None]


def solution(mesh):
    placed = (P(("grp", "tm"), None), P(), P(), P())
    return jax.shard_map(
        per_device,
        mesh=mesh,
        in_specs=placed,
        out_specs=P("spin", ("grp", "tm"), None, "rows"),
        check_vma=False,
    )
```

```python
import functools
import math

import jax
import jax.numpy as jnp
from jax import lax
from jax.experimental import pallas as pl
from jax.experimental.pallas import tpu as pltpu
from jax.sharding import PartitionSpec as P

BF16 = jnp.bfloat16
F32 = jnp.float32
VMEM_BYTES = 48 * 1024 * 1024


def split(x):
    high = x.astype(BF16)
    return high, (x - high.astype(F32)).astype(BF16)


def dot(left, right):
    return jnp.dot(left, right, preferred_element_type=F32)


def cycle_order(tile_cols, n_tiles):
    order = [jnp.int32(0), tile_cols[1, 0]]
    for _ in range(n_tiles - 2):
        here = order[-1]
        order.append(tile_cols[1, here] + tile_cols[2, here] - order[-2])

    def place(tile):
        found = jnp.int32(0)
        for position, name in enumerate(order):
            found = jnp.where(name == tile, jnp.int32(position), found)
        return found

    return order, place


def kinetic_kernel(
    n_tiles, tile_len, hop_scale, chunk, tile_cols, sites, hopping, k_parts, one_hot, w_high, w_low, total
):
    bonds = sites.shape[1]
    pairs = n_tiles // 2
    wide = 2 * tile_len
    order, _ = cycle_order(tile_cols, n_tiles)
    row_ids = lax.broadcasted_iota(jnp.int32, (tile_len, chunk), 0)
    lane_ids = lax.broadcasted_iota(jnp.int32, (tile_len, tile_len), 1)

    def build(begin, slot):
        site_from = sites[0:1, begin : begin + chunk]
        for p in range(n_tiles):
            hits = jnp.where(row_ids + order[p] * tile_len == site_from, 1.0, 0.0).astype(BF16)
            spots = [p + 1]
            if p == n_tiles - 1:
                spots.append(0)
            if p == 0:
                spots.append(n_tiles + 1)
            for spot in spots:
                one_hot[slot, spot * tile_len : (spot + 1) * tile_len, :] = hits
        for part in range(chunk // tile_len):
            at = slice(begin + part * tile_len, begin + (part + 1) * tile_len)
            inside = slice(part * tile_len, (part + 1) * tile_len)
            site_to = jnp.broadcast_to(sites[1:2, at], (tile_len, tile_len)).T
            weight = jnp.broadcast_to(hopping[0:1, at], (tile_len, tile_len)).T
            high = weight.astype(BF16).astype(F32)
            low = weight - high
            for p in range(n_tiles):
                hit = lane_ids + order[p] * tile_len == site_to
                columns = slice(p * tile_len, (p + 1) * tile_len)
                w_high[slot, inside, columns] = jnp.where(hit, high, 0.0).astype(BF16)
                w_low[slot, inside, columns] = jnp.where(hit, low, 0.0).astype(BF16)

    build(0, 0)
    for begin in range(0, bonds, chunk):
        slot = begin // chunk % 2
        if begin + chunk < bonds:
            build(begin + chunk, 1 - slot)
        for r in range(pairs):
            columns = slice(r * wide, (r + 1) * wide)
            found = one_hot[slot, r * wide : (r + 2) * wide, :]
            weights = jnp.concatenate([w_high[slot, :, columns], w_low[slot, :, columns]], axis=0)
            added = dot(jnp.concatenate([found, found], axis=1), weights)
            total[r] = added if begin == 0 else total[r] + added

    def tile_of(p, q):
        r, half = divmod(q, 2)
        row = (p - (2 * r - 1)) % n_tiles
        return r, slice(row * tile_len, (row + 1) * tile_len), slice(half * tile_len, (half + 1) * tile_len)

    diagonal = lax.broadcasted_iota(jnp.int32, (tile_len, tile_len), 0) == lane_ids
    k_parts[...] = jnp.zeros_like(k_parts)
    for q in range(n_tiles):
        for p in ((q - 1) % n_tiles, q, (q + 1) % n_tiles):
            value = hop_scale * (total[tile_of(p, q)] + total[tile_of(q, p)].T)
            if p == q:
                value = jnp.where(diagonal, 1.0, 0.0) + value
            high, low = split(value)
            r, rows, columns = tile_of(p, q)
            for part, piece in enumerate((high, high, low)):
                k_parts[r, part * 2 * wide + rows.start : part * 2 * wide + rows.stop, columns] = piece


def green_kernel(
    n_tiles, tile_len, coupling, width,
    tile_cols, field, k_parts, mine, sent,
    factors, even_high, even_low, odd_high, odd_low, p_high, p_low, a_part, b_part, u_part, p_full, q_full,
):
    total_slices = field.shape[0]
    order_len = n_tiles * tile_len
    pairs = n_tiles // 2
    wide = 2 * tile_len
    order, place = cycle_order(tile_cols, n_tiles)
    strength = (1.0 - 2.0 * lax.axis_index("spin").astype(F32)) * coupling
    for p in range(n_tiles):
        spins_pm = (2 * field[:, pl.ds(pl.multiple_of(order[p] * tile_len, tile_len), tile_len)] - 1).astype(F32)
        factors[:, p * tile_len : (p + 1) * tile_len] = jnp.exp(strength * spins_pm)

    even, odd = (even_high, even_low), (odd_high, odd_low)

    def keep(refs, r, value):
        parts = split(value)
        for ref, part in zip(refs, parts):
            ref[:, tile_len + r * wide : tile_len + (r + 1) * wide] = part
            if r == 0:
                ref[:, tile_len + order_len : 2 * tile_len + order_len] = part[:, :tile_len]
            if r == pairs - 1:
                ref[:, :tile_len] = part[:, tile_len:]

    for r in range(pairs):
        window = k_parts[r, : 2 * wide].astype(F32) + k_parts[r, 4 * wide :].astype(F32)
        rows = [jnp.zeros((tile_len, wide), F32)] * n_tiles
        for row in range(4):
            rows[(2 * r - 1 + row) % n_tiles] = window[row * tile_len : (row + 1) * tile_len]
        keep(even, r, jnp.concatenate(rows, axis=0) * factors[0:1, r * wide : (r + 1) * wide])

    def multiplied(refs, step, r):
        window = slice(r * wide, (r + 2) * wide)
        high = refs[0][:, window]
        value = dot(jnp.concatenate([high, refs[1][:, window], high], axis=1), k_parts[r])
        return value * factors[pl.ds(step, 1), r * wide : (r + 1) * wide]

    def two_steps(pair, carry):
        step = 2 * pair + 1
        for r in range(pairs):
            keep(odd, r, multiplied(even, step, r))
        for r in range(pairs):
            keep(even, r, multiplied(odd, step + 1, r))
        return carry

    lax.fori_loop(0, (total_slices - 2) // 2, two_steps, 0)
    newest = even
    if total_slices % 2:
        for r in range(pairs):
            keep(odd, r, multiplied(even, total_slices - 2, r))
        newest = odd
    for r in range(pairs):
        p_full[:, r * wide : (r + 1) * wide] = multiplied(newest, total_slices - 1, r)
    inner = slice(tile_len, tile_len + order_len)
    product = p_full[...]
    col_max = jnp.max(jnp.sum(product, axis=1))
    power = product * (0.5 / col_max)
    p_full[...] = power
    high, low = split(power)
    p_high[...] = high
    p_low[...] = low

    bands = [slice(r * wide, (r + 1) * wide) for r in range(pairs)]
    for band in bands:
        value = dot(p_high[...], p_high[:, band])
        a_part[:, band] = value.astype(BF16)
        value -= p_full[:, band]
        q_full[:, band] = value
        u_part[:, band] = value.astype(BF16)
    for band in bands:
        value = -dot(p_high[...], a_part[:, band])
        b_part[:, band] = value.astype(BF16)
    for band in bands:
        value = b_part[:, band].astype(F32) + dot(b_part[...], b_part[:, band])
        q_full[:, band] += value
        a_part[:, band] = value.astype(BF16)
    q_high, q_low = even_high.at[:, inner], even_low.at[:, inner]
    for band in bands:
        value = -(q_full[:, band] + dot(u_part[...], a_part[:, band]))
        q_full[:, band] = value
        q_high[:, band], q_low[:, band] = split(value)
    for band in bands:
        left = jnp.concatenate([p_high[...], p_low[...], p_high[...]], axis=1)
        right = jnp.concatenate([q_high[:, band], q_high[:, band], q_low[:, band]], axis=0)
        residual = dot(left, right) + (q_full[:, band] - p_full[:, band])
        a_part[:, band] = residual.astype(BF16)
        q_full[:, band] -= residual
    for band in bands:
        q_full[:, band] += dot(q_high[...], a_part[:, band])

    base = lax.axis_index("rows") * (width // tile_len) if width < order_len else jnp.int32(0)
    tile = (tile_len, tile_len)
    diagonal = lax.broadcasted_iota(jnp.int32, tile, 0) == lax.broadcasted_iota(jnp.int32, tile, 1)
    spots = [pl.multiple_of(place(jnp.int32(a)) * tile_len, tile_len) for a in range(n_tiles)]
    for b in range(width // tile_len):
        spot = pl.multiple_of(place(base + b) * tile_len, tile_len)
        columns = slice(b * tile_len, (b + 1) * tile_len)
        for a in range(n_tiles):
            rows = slice(a * tile_len, (a + 1) * tile_len)
            sent[rows, columns] = q_full[pl.ds(spots[a], tile_len), pl.ds(spot, tile_len)]
            unit = jnp.where(diagonal & (base + b == a), 1.0, 0.0)
            mine[rows, columns] = unit - q_full[pl.ds(spot, tile_len), pl.ds(spots[a], tile_len)].T


def per_device(ising_field, bond_sites, hopping, tile_cols):
    slices_here, matrix_order = ising_field.shape
    n_tiles = tile_cols.shape[0]
    tile_len = matrix_order // n_tiles
    bonds = bond_sites.shape[0]
    n_rows = lax.axis_size("rows")
    col_width = matrix_order // n_rows
    total_slices = slices_here * lax.axis_size("tm")
    pairs = n_tiles // 2
    wide = 2 * tile_len
    extended = matrix_order + wide
    vmem = pl.BlockSpec(memory_space=pltpu.VMEM)
    smem = pl.BlockSpec(memory_space=pltpu.SMEM)
    square = (matrix_order, matrix_order)
    n_time = lax.axis_size("tm")
    blocks = [ising_field]
    for ahead in range(1, n_time):
        blocks.append(lax.ppermute(ising_field, "tm", [(i, (i - ahead) % n_time) for i in range(n_time)]))
    field = jnp.concatenate(blocks, axis=0)
    chunk = 4 * tile_len
    k_parts = pl.pallas_call(
        functools.partial(kinetic_kernel, n_tiles, tile_len, 0.5 / total_slices, chunk),
        out_shape=jax.ShapeDtypeStruct((pairs, 6 * wide, wide), BF16),
        in_specs=[smem, vmem, vmem],
        out_specs=vmem,
        scratch_shapes=[
            pltpu.VMEM((2, extended, chunk), BF16),
            pltpu.VMEM((2, chunk, matrix_order), BF16),
            pltpu.VMEM((2, chunk, matrix_order), BF16),
            pltpu.VMEM((pairs, 2 * wide, wide), F32),
        ],
        compiler_params=pltpu.CompilerParams(vmem_limit_bytes=VMEM_BYTES),
        cost_estimate=pl.CostEstimate(
            flops=4 * bonds * 2 * matrix_order * wide, bytes_accessed=4 * matrix_order * wide, transcendentals=0
        ),
        name="kinetic",
    )(tile_cols.T, bond_sites.T, hopping[None, :])
    width = col_width if col_width % tile_len == 0 else matrix_order
    half = jax.ShapeDtypeStruct((matrix_order, width), F32)
    mine, sent = pl.pallas_call(
        functools.partial(
            green_kernel, n_tiles, tile_len, 1.5 / math.sqrt(total_slices), width
        ),
        out_shape=(half, half),
        in_specs=[smem, vmem, vmem],
        out_specs=(vmem, vmem),
        scratch_shapes=[pltpu.VMEM((total_slices, matrix_order), F32)]
        + [pltpu.VMEM((matrix_order, extended), BF16)] * 4
        + [pltpu.VMEM(square, BF16)] * 5
        + [pltpu.VMEM(square, F32)] * 2,
        compiler_params=pltpu.CompilerParams(vmem_limit_bytes=VMEM_BYTES),
        cost_estimate=pl.CostEstimate(
            flops=6 * total_slices * matrix_order * 2 * matrix_order * wide + 16 * matrix_order**3,
            bytes_accessed=8 * matrix_order * matrix_order,
            transcendentals=total_slices * matrix_order,
        ),
        name="green",
    )(tile_cols.T, field, k_parts)
    offset = lax.axis_index("rows") * col_width
    if width != col_width:
        mine = lax.dynamic_slice_in_dim(mine, offset, col_width, 1)
        sent = lax.dynamic_slice_in_dim(sent, offset, col_width, 1)
    n_spin = lax.axis_size("spin")
    other = lax.ppermute(sent, "spin", [(i, n_spin - 1 - i) for i in range(n_spin)])
    xcorr = mine * other
    return xcorr[None, None]


def solution(mesh):
    placed = (P(("grp", "tm"), None), P(), P(), P())
    return jax.shard_map(
        per_device,
        mesh=mesh,
        in_specs=placed,
        out_specs=P("spin", ("grp", "tm"), None, "rows"),
        check_vma=False,
    )
```

```python
import functools
import math

import jax
import jax.numpy as jnp
from jax import lax
from jax.experimental import pallas as pl
from jax.experimental.pallas import tpu as pltpu
from jax.sharding import PartitionSpec as P

BF16 = jnp.bfloat16
F32 = jnp.float32
VMEM_BYTES = 48 * 1024 * 1024
MESH = pl.DeviceIdType.MESH


def split(x):
    high = x.astype(BF16)
    return high, (x - high.astype(F32)).astype(BF16)


def dot(left, right):
    return jnp.dot(left, right, preferred_element_type=F32)


def cycle_order(tile_cols, n_tiles):
    order = [jnp.int32(0), tile_cols[1, 0]]
    for _ in range(n_tiles - 2):
        here = order[-1]
        order.append(tile_cols[1, here] + tile_cols[2, here] - order[-2])

    def place(tile):
        found = jnp.int32(0)
        for position, name in enumerate(order):
            found = jnp.where(name == tile, jnp.int32(position), found)
        return found

    return order, place


def kinetic_kernel(
    n_tiles, tile_len, hop_scale, chunk, n_time, tile_cols, sites, hopping, field, k_parts, circle,
    one_hot, w_high, w_low, total, landed, send_sems, recv_sems
):
    me = lax.axis_index("tm")
    barrier = pltpu.get_barrier_semaphore()
    for ahead in range(1, n_time):
        peer = lax.rem(me + ahead, n_time)
        pl.semaphore_signal(barrier, inc=1, device_id={"tm": peer}, device_id_type=MESH)
    bonds = sites.shape[1]
    pairs = n_tiles // 2
    wide = 2 * tile_len
    order, _ = cycle_order(tile_cols, n_tiles)
    row_ids = lax.broadcasted_iota(jnp.int32, (tile_len, chunk), 0)
    lane_ids = lax.broadcasted_iota(jnp.int32, (tile_len, tile_len), 1)

    def build(begin, slot):
        site_from = sites[0:1, begin : begin + chunk]
        for p in range(n_tiles):
            hits = jnp.where(row_ids + order[p] * tile_len == site_from, 1.0, 0.0).astype(BF16)
            spots = [p + 1]
            if p == n_tiles - 1:
                spots.append(0)
            if p == 0:
                spots.append(n_tiles + 1)
            for spot in spots:
                one_hot[slot, spot * tile_len : (spot + 1) * tile_len, :] = hits
        for part in range(chunk // tile_len):
            at = slice(begin + part * tile_len, begin + (part + 1) * tile_len)
            inside = slice(part * tile_len, (part + 1) * tile_len)
            site_to = jnp.broadcast_to(sites[1:2, at], (tile_len, tile_len)).T
            weight = jnp.broadcast_to(hopping[0:1, at], (tile_len, tile_len)).T
            high = weight.astype(BF16).astype(F32)
            low = weight - high
            for p in range(n_tiles):
                hit = lane_ids + order[p] * tile_len == site_to
                columns = slice(p * tile_len, (p + 1) * tile_len)
                w_high[slot, inside, columns] = jnp.where(hit, high, 0.0).astype(BF16)
                w_low[slot, inside, columns] = jnp.where(hit, low, 0.0).astype(BF16)

    build(0, 0)
    copies = []
    for begin in range(0, bonds, chunk):
        if begin == chunk:
            pl.semaphore_wait(barrier, n_time - 1)
            for ahead in range(1, n_time):
                copies.append(
                    pltpu.make_async_remote_copy(
                        src_ref=field,
                        dst_ref=landed.at[ahead],
                        send_sem=send_sems.at[ahead],
                        recv_sem=recv_sems.at[ahead],
                        device_id={"tm": lax.rem(me + n_time - ahead, n_time)},
                        device_id_type=MESH,
                    )
                )
                copies[-1].start()
        slot = begin // chunk % 2
        if begin + chunk < bonds:
            build(begin + chunk, 1 - slot)
        for r in range(pairs):
            columns = slice(r * wide, (r + 1) * wide)
            found = one_hot[slot, r * wide : (r + 2) * wide, :]
            weights = jnp.concatenate([w_high[slot, :, columns], w_low[slot, :, columns]], axis=0)
            added = dot(jnp.concatenate([found, found], axis=1), weights)
            total[r] = added if begin == 0 else total[r] + added

    def tile_of(p, q):
        r, half = divmod(q, 2)
        row = (p - (2 * r - 1)) % n_tiles
        return r, slice(row * tile_len, (row + 1) * tile_len), slice(half * tile_len, (half + 1) * tile_len)

    diagonal = lax.broadcasted_iota(jnp.int32, (tile_len, tile_len), 0) == lane_ids
    k_parts[...] = jnp.zeros_like(k_parts)
    for q in range(n_tiles):
        for p in ((q - 1) % n_tiles, q, (q + 1) % n_tiles):
            value = hop_scale * (total[tile_of(p, q)] + total[tile_of(q, p)].T)
            if p == q:
                value = jnp.where(diagonal, 1.0, 0.0) + value
            high, low = split(value)
            r, rows, columns = tile_of(p, q)
            for part, piece in enumerate((high, high, low)):
                k_parts[r, part * 2 * wide + rows.start : part * 2 * wide + rows.stop, columns] = piece
    for copy in copies:
        copy.wait()
    slices_here = field.shape[0]
    for ahead in range(n_time):
        block = field[...] if ahead == 0 else landed[ahead]
        circle[ahead * slices_here : (ahead + 1) * slices_here, :] = block


def green_kernel(
    n_tiles, tile_len, coupling, width,
    tile_cols, field, k_parts, mine, sent,
    factors, even_high, even_low, odd_high, odd_low, p_high, p_low, a_part, b_part, u_part, p_full, q_full,
):
    total_slices = field.shape[0]
    order_len = n_tiles * tile_len
    pairs = n_tiles // 2
    wide = 2 * tile_len
    order, place = cycle_order(tile_cols, n_tiles)
    strength = (1.0 - 2.0 * lax.axis_index("spin").astype(F32)) * coupling
    for p in range(n_tiles):
        spins_pm = (2 * field[:, pl.ds(pl.multiple_of(order[p] * tile_len, tile_len), tile_len)] - 1).astype(F32)
        factors[:, p * tile_len : (p + 1) * tile_len] = jnp.exp(strength * spins_pm)

    even, odd = (even_high, even_low), (odd_high, odd_low)

    def keep(refs, r, value):
        parts = split(value)
        for ref, part in zip(refs, parts):
            ref[:, tile_len + r * wide : tile_len + (r + 1) * wide] = part
            if r == 0:
                ref[:, tile_len + order_len : 2 * tile_len + order_len] = part[:, :tile_len]
            if r == pairs - 1:
                ref[:, :tile_len] = part[:, tile_len:]

    for r in range(pairs):
        window = k_parts[r, : 2 * wide].astype(F32) + k_parts[r, 4 * wide :].astype(F32)
        rows = [jnp.zeros((tile_len, wide), F32)] * n_tiles
        for row in range(4):
            rows[(2 * r - 1 + row) % n_tiles] = window[row * tile_len : (row + 1) * tile_len]
        keep(even, r, jnp.concatenate(rows, axis=0) * factors[0:1, r * wide : (r + 1) * wide])

    def multiplied(refs, step, r):
        window = slice(r * wide, (r + 2) * wide)
        high = refs[0][:, window]
        value = dot(jnp.concatenate([high, refs[1][:, window], high], axis=1), k_parts[r])
        return value * factors[pl.ds(step, 1), r * wide : (r + 1) * wide]

    def two_steps(pair, carry):
        step = 2 * pair + 1
        for r in range(pairs):
            keep(odd, r, multiplied(even, step, r))
        for r in range(pairs):
            keep(even, r, multiplied(odd, step + 1, r))
        return carry

    lax.fori_loop(0, (total_slices - 2) // 2, two_steps, 0)
    newest = even
    if total_slices % 2:
        for r in range(pairs):
            keep(odd, r, multiplied(even, total_slices - 2, r))
        newest = odd
    for r in range(pairs):
        p_full[:, r * wide : (r + 1) * wide] = multiplied(newest, total_slices - 1, r)
    inner = slice(tile_len, tile_len + order_len)
    product = p_full[...]
    col_max = jnp.max(jnp.sum(product, axis=1))
    power = product * (0.5 / col_max)
    p_full[...] = power
    high, low = split(power)
    p_high[...] = high
    p_low[...] = low

    bands = [slice(r * wide, (r + 1) * wide) for r in range(pairs)]
    for band in bands:
        value = dot(p_high[...], p_high[:, band])
        a_part[:, band] = value.astype(BF16)
        value -= p_full[:, band]
        q_full[:, band] = value
        u_part[:, band] = value.astype(BF16)
    for band in bands:
        value = -dot(p_high[...], a_part[:, band])
        b_part[:, band] = value.astype(BF16)
    for band in bands:
        value = b_part[:, band].astype(F32) + dot(b_part[...], b_part[:, band])
        q_full[:, band] += value
        a_part[:, band] = value.astype(BF16)
    q_high, q_low = even_high.at[:, inner], even_low.at[:, inner]
    for band in bands:
        value = -(q_full[:, band] + dot(u_part[...], a_part[:, band]))
        q_full[:, band] = value
        q_high[:, band], q_low[:, band] = split(value)
    for band in bands:
        left = jnp.concatenate([p_high[...], p_low[...], p_high[...]], axis=1)
        right = jnp.concatenate([q_high[:, band], q_high[:, band], q_low[:, band]], axis=0)
        residual = dot(left, right) + (q_full[:, band] - p_full[:, band])
        a_part[:, band] = residual.astype(BF16)
        q_full[:, band] -= residual
    for band in bands:
        q_full[:, band] += dot(q_high[...], a_part[:, band])

    base = lax.axis_index("rows") * (width // tile_len) if width < order_len else jnp.int32(0)
    tile = (tile_len, tile_len)
    diagonal = lax.broadcasted_iota(jnp.int32, tile, 0) == lax.broadcasted_iota(jnp.int32, tile, 1)
    spots = [pl.multiple_of(place(jnp.int32(a)) * tile_len, tile_len) for a in range(n_tiles)]
    for b in range(width // tile_len):
        spot = pl.multiple_of(place(base + b) * tile_len, tile_len)
        columns = slice(b * tile_len, (b + 1) * tile_len)
        for a in range(n_tiles):
            rows = slice(a * tile_len, (a + 1) * tile_len)
            sent[rows, columns] = q_full[pl.ds(spots[a], tile_len), pl.ds(spot, tile_len)]
            unit = jnp.where(diagonal & (base + b == a), 1.0, 0.0)
            mine[rows, columns] = unit - q_full[pl.ds(spot, tile_len), pl.ds(spots[a], tile_len)].T


def per_device(ising_field, bond_sites, hopping, tile_cols):
    slices_here, matrix_order = ising_field.shape
    n_tiles = tile_cols.shape[0]
    tile_len = matrix_order // n_tiles
    bonds = bond_sites.shape[0]
    n_rows = lax.axis_size("rows")
    col_width = matrix_order // n_rows
    total_slices = slices_here * lax.axis_size("tm")
    pairs = n_tiles // 2
    wide = 2 * tile_len
    extended = matrix_order + wide
    vmem = pl.BlockSpec(memory_space=pltpu.VMEM)
    smem = pl.BlockSpec(memory_space=pltpu.SMEM)
    square = (matrix_order, matrix_order)
    n_time = lax.axis_size("tm")
    chunk = 4 * tile_len
    k_parts, circle = pl.pallas_call(
        functools.partial(kinetic_kernel, n_tiles, tile_len, 0.5 / total_slices, chunk, n_time),
        out_shape=(
            jax.ShapeDtypeStruct((pairs, 6 * wide, wide), BF16),
            jax.ShapeDtypeStruct((total_slices, matrix_order), jnp.int32),
        ),
        in_specs=[smem, vmem, vmem, vmem],
        out_specs=(vmem, vmem),
        scratch_shapes=[
            pltpu.VMEM((2, extended, chunk), BF16),
            pltpu.VMEM((2, chunk, matrix_order), BF16),
            pltpu.VMEM((2, chunk, matrix_order), BF16),
            pltpu.VMEM((pairs, 2 * wide, wide), F32),
            pltpu.VMEM((n_time, slices_here, matrix_order), jnp.int32),
            pltpu.SemaphoreType.DMA((n_time,)),
            pltpu.SemaphoreType.DMA((n_time,)),
        ],
        compiler_params=pltpu.CompilerParams(
            vmem_limit_bytes=VMEM_BYTES, collective_id=0, has_side_effects=True
        ),
        cost_estimate=pl.CostEstimate(
            flops=4 * bonds * 2 * matrix_order * wide, bytes_accessed=4 * matrix_order * wide, transcendentals=0
        ),
        name="kinetic",
    )(tile_cols.T, bond_sites.T, hopping[None, :], ising_field)
    width = col_width if col_width % tile_len == 0 else matrix_order
    half = jax.ShapeDtypeStruct((matrix_order, width), F32)
    mine, sent = pl.pallas_call(
        functools.partial(
            green_kernel, n_tiles, tile_len, 1.5 / math.sqrt(total_slices), width
        ),
        out_shape=(half, half),
        in_specs=[smem, vmem, vmem],
        out_specs=(vmem, vmem),
        scratch_shapes=[pltpu.VMEM((total_slices, matrix_order), F32)]
        + [pltpu.VMEM((matrix_order, extended), BF16)] * 4
        + [pltpu.VMEM(square, BF16)] * 5
        + [pltpu.VMEM(square, F32)] * 2,
        compiler_params=pltpu.CompilerParams(vmem_limit_bytes=VMEM_BYTES),
        cost_estimate=pl.CostEstimate(
            flops=6 * total_slices * matrix_order * 2 * matrix_order * wide + 16 * matrix_order**3,
            bytes_accessed=8 * matrix_order * matrix_order,
            transcendentals=total_slices * matrix_order,
        ),
        name="green",
    )(tile_cols.T, circle, k_parts)
    offset = lax.axis_index("rows") * col_width
    if width != col_width:
        mine = lax.dynamic_slice_in_dim(mine, offset, col_width, 1)
        sent = lax.dynamic_slice_in_dim(sent, offset, col_width, 1)
    n_spin = lax.axis_size("spin")
    other = lax.ppermute(sent, "spin", [(i, n_spin - 1 - i) for i in range(n_spin)])
    xcorr = mine * other
    return xcorr[None, None]


def solution(mesh):
    placed = (P(("grp", "tm"), None), P(), P(), P())
    return jax.shard_map(
        per_device,
        mesh=mesh,
        in_specs=placed,
        out_specs=P("spin", ("grp", "tm"), None, "rows"),
        check_vma=False,
    )
```

```python
import functools
import math

import jax
import jax.numpy as jnp
from jax import lax
from jax.experimental import pallas as pl
from jax.experimental.pallas import tpu as pltpu
from jax.sharding import PartitionSpec as P

BF16 = jnp.bfloat16
F32 = jnp.float32
VMEM_BYTES = 48 * 1024 * 1024
MESH = pl.DeviceIdType.MESH


def split(x):
    high = x.astype(BF16)
    return high, (x - high.astype(F32)).astype(BF16)


def dot(left, right):
    return jnp.dot(left, right, preferred_element_type=F32)


def cycle_order(tile_cols, n_tiles):
    order = [jnp.int32(0), tile_cols[1, 0]]
    for _ in range(n_tiles - 2):
        here = order[-1]
        order.append(tile_cols[1, here] + tile_cols[2, here] - order[-2])

    def place(tile):
        found = jnp.int32(0)
        for position, name in enumerate(order):
            found = jnp.where(name == tile, jnp.int32(position), found)
        return found

    return order, place


def kinetic_kernel(
    n_tiles, tile_len, hop_scale, chunk, n_time, tile_cols, sites, hopping, field, k_parts, circle,
    one_hot, w_high, w_low, total, landed, send_sems, recv_sems
):
    me = lax.axis_index("tm")
    barrier = pltpu.get_barrier_semaphore()
    for ahead in range(1, n_time):
        peer = lax.rem(me + ahead, n_time)
        pl.semaphore_signal(barrier, inc=1, device_id={"tm": peer}, device_id_type=MESH)
    bonds = sites.shape[1]
    pairs = n_tiles // 2
    wide = 2 * tile_len
    order, _ = cycle_order(tile_cols, n_tiles)
    row_ids = lax.broadcasted_iota(jnp.int32, (tile_len, chunk), 0)
    lane_ids = lax.broadcasted_iota(jnp.int32, (tile_len, tile_len), 1)

    def build(begin, slot):
        site_from = sites[0:1, begin : begin + chunk]
        for p in range(n_tiles):
            hits = jnp.where(row_ids + order[p] * tile_len == site_from, 1.0, 0.0).astype(BF16)
            spots = [p + 1]
            if p == n_tiles - 1:
                spots.append(0)
            if p == 0:
                spots.append(n_tiles + 1)
            for spot in spots:
                one_hot[slot, spot * tile_len : (spot + 1) * tile_len, :] = hits
        for part in range(chunk // tile_len):
            at = slice(begin + part * tile_len, begin + (part + 1) * tile_len)
            inside = slice(part * tile_len, (part + 1) * tile_len)
            site_to = jnp.broadcast_to(sites[1:2, at], (tile_len, tile_len)).T
            weight = jnp.broadcast_to(hopping[0:1, at], (tile_len, tile_len)).T
            high = weight.astype(BF16).astype(F32)
            low = weight - high
            for p in range(n_tiles):
                hit = lane_ids + order[p] * tile_len == site_to
                columns = slice(p * tile_len, (p + 1) * tile_len)
                w_high[slot, inside, columns] = jnp.where(hit, high, 0.0).astype(BF16)
                w_low[slot, inside, columns] = jnp.where(hit, low, 0.0).astype(BF16)

    build(0, 0)
    copies = []
    send_at = bonds // chunk * 2 // 3 * chunk
    for begin in range(0, bonds, chunk):
        if begin == send_at:
            pl.semaphore_wait(barrier, n_time - 1)
            for ahead in range(1, n_time):
                copies.append(
                    pltpu.make_async_remote_copy(
                        src_ref=field,
                        dst_ref=landed.at[ahead],
                        send_sem=send_sems.at[ahead],
                        recv_sem=recv_sems.at[ahead],
                        device_id={"tm": lax.rem(me + n_time - ahead, n_time)},
                        device_id_type=MESH,
                    )
                )
                copies[-1].start()
        slot = begin // chunk % 2
        if begin + chunk < bonds:
            build(begin + chunk, 1 - slot)
        for r in range(pairs):
            columns = slice(r * wide, (r + 1) * wide)
            found = one_hot[slot, r * wide : (r + 2) * wide, :]
            weights = jnp.concatenate([w_high[slot, :, columns], w_low[slot, :, columns]], axis=0)
            added = dot(jnp.concatenate([found, found], axis=1), weights)
            total[r] = added if begin == 0 else total[r] + added

    def tile_of(p, q):
        r, half = divmod(q, 2)
        row = (p - (2 * r - 1)) % n_tiles
        return r, slice(row * tile_len, (row + 1) * tile_len), slice(half * tile_len, (half + 1) * tile_len)

    diagonal = lax.broadcasted_iota(jnp.int32, (tile_len, tile_len), 0) == lane_ids
    k_parts[...] = jnp.zeros_like(k_parts)
    for q in range(n_tiles):
        for p in ((q - 1) % n_tiles, q, (q + 1) % n_tiles):
            value = hop_scale * (total[tile_of(p, q)] + total[tile_of(q, p)].T)
            if p == q:
                value = jnp.where(diagonal, 1.0, 0.0) + value
            high, low = split(value)
            r, rows, columns = tile_of(p, q)
            for part, piece in enumerate((high, high, low)):
                k_parts[r, part * 2 * wide + rows.start : part * 2 * wide + rows.stop, columns] = piece
    for copy in copies:
        copy.wait()
    slices_here = field.shape[0]
    for ahead in range(n_time):
        block = field[...] if ahead == 0 else landed[ahead]
        circle[ahead * slices_here : (ahead + 1) * slices_here, :] = block


def green_kernel(
    n_tiles, tile_len, coupling, width,
    tile_cols, field, k_parts, mine, sent,
    factors, even_high, even_low, odd_high, odd_low, p_high, p_low, a_part, b_part, u_part, p_full, q_full,
):
    total_slices = field.shape[0]
    order_len = n_tiles * tile_len
    pairs = n_tiles // 2
    wide = 2 * tile_len
    order, place = cycle_order(tile_cols, n_tiles)
    strength = (1.0 - 2.0 * lax.axis_index("spin").astype(F32)) * coupling
    for p in range(n_tiles):
        spins_pm = (2 * field[:, pl.ds(pl.multiple_of(order[p] * tile_len, tile_len), tile_len)] - 1).astype(F32)
        factors[:, p * tile_len : (p + 1) * tile_len] = jnp.exp(strength * spins_pm)

    even, odd = (even_high, even_low), (odd_high, odd_low)

    def keep(refs, r, value):
        parts = split(value)
        for ref, part in zip(refs, parts):
            ref[:, tile_len + r * wide : tile_len + (r + 1) * wide] = part
            if r == 0:
                ref[:, tile_len + order_len : 2 * tile_len + order_len] = part[:, :tile_len]
            if r == pairs - 1:
                ref[:, :tile_len] = part[:, tile_len:]

    for r in range(pairs):
        window = k_parts[r, : 2 * wide].astype(F32) + k_parts[r, 4 * wide :].astype(F32)
        rows = [jnp.zeros((tile_len, wide), F32)] * n_tiles
        for row in range(4):
            rows[(2 * r - 1 + row) % n_tiles] = window[row * tile_len : (row + 1) * tile_len]
        keep(even, r, jnp.concatenate(rows, axis=0) * factors[0:1, r * wide : (r + 1) * wide])

    def multiplied(refs, step, r):
        window = slice(r * wide, (r + 2) * wide)
        high = refs[0][:, window]
        value = dot(jnp.concatenate([high, refs[1][:, window], high], axis=1), k_parts[r])
        return value * factors[pl.ds(step, 1), r * wide : (r + 1) * wide]

    def two_steps(pair, carry):
        step = 2 * pair + 1
        for r in range(pairs):
            keep(odd, r, multiplied(even, step, r))
        for r in range(pairs):
            keep(even, r, multiplied(odd, step + 1, r))
        return carry

    lax.fori_loop(0, (total_slices - 2) // 2, two_steps, 0)
    newest = even
    if total_slices % 2:
        for r in range(pairs):
            keep(odd, r, multiplied(even, total_slices - 2, r))
        newest = odd
    for r in range(pairs):
        p_full[:, r * wide : (r + 1) * wide] = multiplied(newest, total_slices - 1, r)
    inner = slice(tile_len, tile_len + order_len)
    product = p_full[...]
    col_max = jnp.max(jnp.sum(product, axis=1))
    power = product * (0.5 / col_max)
    p_full[...] = power
    high, low = split(power)
    p_high[...] = high
    p_low[...] = low

    bands = [slice(r * wide, (r + 1) * wide) for r in range(pairs)]
    for band in bands:
        value = dot(p_high[...], p_high[:, band])
        a_part[:, band] = value.astype(BF16)
        value -= p_full[:, band]
        q_full[:, band] = value
        u_part[:, band] = value.astype(BF16)
    for band in bands:
        value = -dot(p_high[...], a_part[:, band])
        b_part[:, band] = value.astype(BF16)
    for band in bands:
        value = b_part[:, band].astype(F32) + dot(b_part[...], b_part[:, band])
        q_full[:, band] += value
        a_part[:, band] = value.astype(BF16)
    q_high, q_low = even_high.at[:, inner], even_low.at[:, inner]
    for band in bands:
        value = -(q_full[:, band] + dot(u_part[...], a_part[:, band]))
        q_full[:, band] = value
        q_high[:, band], q_low[:, band] = split(value)
    for band in bands:
        left = jnp.concatenate([p_high[...], p_low[...], p_high[...]], axis=1)
        right = jnp.concatenate([q_high[:, band], q_high[:, band], q_low[:, band]], axis=0)
        residual = dot(left, right) + (q_full[:, band] - p_full[:, band])
        a_part[:, band] = residual.astype(BF16)
        q_full[:, band] -= residual
    for band in bands:
        q_full[:, band] += dot(q_high[...], a_part[:, band])

    base = lax.axis_index("rows") * (width // tile_len) if width < order_len else jnp.int32(0)
    tile = (tile_len, tile_len)
    diagonal = lax.broadcasted_iota(jnp.int32, tile, 0) == lax.broadcasted_iota(jnp.int32, tile, 1)
    spots = [pl.multiple_of(place(jnp.int32(a)) * tile_len, tile_len) for a in range(n_tiles)]
    for b in range(width // tile_len):
        spot = pl.multiple_of(place(base + b) * tile_len, tile_len)
        columns = slice(b * tile_len, (b + 1) * tile_len)
        for a in range(n_tiles):
            rows = slice(a * tile_len, (a + 1) * tile_len)
            sent[rows, columns] = q_full[pl.ds(spots[a], tile_len), pl.ds(spot, tile_len)]
            unit = jnp.where(diagonal & (base + b == a), 1.0, 0.0)
            mine[rows, columns] = unit - q_full[pl.ds(spot, tile_len), pl.ds(spots[a], tile_len)].T


def per_device(ising_field, bond_sites, hopping, tile_cols):
    slices_here, matrix_order = ising_field.shape
    n_tiles = tile_cols.shape[0]
    tile_len = matrix_order // n_tiles
    bonds = bond_sites.shape[0]
    n_rows = lax.axis_size("rows")
    col_width = matrix_order // n_rows
    total_slices = slices_here * lax.axis_size("tm")
    pairs = n_tiles // 2
    wide = 2 * tile_len
    extended = matrix_order + wide
    vmem = pl.BlockSpec(memory_space=pltpu.VMEM)
    smem = pl.BlockSpec(memory_space=pltpu.SMEM)
    square = (matrix_order, matrix_order)
    n_time = lax.axis_size("tm")
    chunk = 4 * tile_len
    k_parts, circle = pl.pallas_call(
        functools.partial(kinetic_kernel, n_tiles, tile_len, 0.5 / total_slices, chunk, n_time),
        out_shape=(
            jax.ShapeDtypeStruct((pairs, 6 * wide, wide), BF16),
            jax.ShapeDtypeStruct((total_slices, matrix_order), jnp.int32),
        ),
        in_specs=[smem, vmem, vmem, vmem],
        out_specs=(vmem, vmem),
        scratch_shapes=[
            pltpu.VMEM((2, extended, chunk), BF16),
            pltpu.VMEM((2, chunk, matrix_order), BF16),
            pltpu.VMEM((2, chunk, matrix_order), BF16),
            pltpu.VMEM((pairs, 2 * wide, wide), F32),
            pltpu.VMEM((n_time, slices_here, matrix_order), jnp.int32),
            pltpu.SemaphoreType.DMA((n_time,)),
            pltpu.SemaphoreType.DMA((n_time,)),
        ],
        compiler_params=pltpu.CompilerParams(
            vmem_limit_bytes=VMEM_BYTES, collective_id=0, has_side_effects=True
        ),
        cost_estimate=pl.CostEstimate(
            flops=4 * bonds * 2 * matrix_order * wide, bytes_accessed=4 * matrix_order * wide, transcendentals=0
        ),
        name="kinetic",
    )(tile_cols.T, bond_sites.T, hopping[None, :], ising_field)
    width = col_width if col_width % tile_len == 0 else matrix_order
    half = jax.ShapeDtypeStruct((matrix_order, width), F32)
    mine, sent = pl.pallas_call(
        functools.partial(
            green_kernel, n_tiles, tile_len, 1.5 / math.sqrt(total_slices), width
        ),
        out_shape=(half, half),
        in_specs=[smem, vmem, vmem],
        out_specs=(vmem, vmem),
        scratch_shapes=[pltpu.VMEM((total_slices, matrix_order), F32)]
        + [pltpu.VMEM((matrix_order, extended), BF16)] * 4
        + [pltpu.VMEM(square, BF16)] * 5
        + [pltpu.VMEM(square, F32)] * 2,
        compiler_params=pltpu.CompilerParams(vmem_limit_bytes=VMEM_BYTES),
        cost_estimate=pl.CostEstimate(
            flops=6 * total_slices * matrix_order * 2 * matrix_order * wide + 16 * matrix_order**3,
            bytes_accessed=8 * matrix_order * matrix_order,
            transcendentals=total_slices * matrix_order,
        ),
        name="green",
    )(tile_cols.T, circle, k_parts)
    offset = lax.axis_index("rows") * col_width
    if width != col_width:
        mine = lax.dynamic_slice_in_dim(mine, offset, col_width, 1)
        sent = lax.dynamic_slice_in_dim(sent, offset, col_width, 1)
    n_spin = lax.axis_size("spin")
    other = lax.ppermute(sent, "spin", [(i, n_spin - 1 - i) for i in range(n_spin)])
    xcorr = mine * other
    return xcorr[None, None]


def solution(mesh):
    placed = (P(("grp", "tm"), None), P(), P(), P())
    return jax.shard_map(
        per_device,
        mesh=mesh,
        in_specs=placed,
        out_specs=P("spin", ("grp", "tm"), None, "rows"),
        check_vma=False,
    )
```
